32 devices in a mesh: section: 8 (over z, y), dom: 4 (over x, core).
Axes of the slice: x: 2, y: 2, z: 4, core: 2. Of those that a mesh axis runs over, the one named last changes fastest.
Arguments:
- features: bfloat16 [12, 1024, 256], P(None, 'dom'), may hold values from -6 to 6
- cotangent: bfloat16 [12, 1024, 256], P(None, 'dom'), may hold values from -3 to 3
- weights: bfloat16 [8, 256, 256], P('section'), may hold values from -0.375 to 0.375
- tiles: bfloat16 [8, 6, 128, 128], P('dom'), may hold values from 0.0005 to 1
- sources: int32 [8, 6], P('dom'), may hold values from 0 to 7, as said below
- counts: int32 [8], P('dom'), may hold values from 1 to 6
Outputs:
- weight_grads: float32 [8, 256, 256], P('section')
The draws below stay inside these ranges and needn't reach their ends.
Inputs may be any that keep to these rules, and one draw needn't show every extreme that they name: `sources`: entry 0 of each block's list is the block itself; every entry, used or not, names a block that lies on the same index of dom or is the block just before or just after that index's blocks.
All inputs are finite; a program needn't handle non-finite values.
Results may differ from the reference program's by a relative error of at most 0.02.
Values may be sent and summed in bfloat16 or wider, within the bound.
No kernel may reach another device: no remote copies, remote signals or barrier semaphores. Data moves between devices by JAX's collectives and lax.ppermute only.
A program may use at most 64 MiB of HBM per device.

```python
import math
import jax
import jax.numpy as jnp
from jax import lax

HID = 256
BS = 128
KNB = 6
BLK_DEV = 2
MB = 12
LAYERS = 8
NBLK = 8
NODES = 1024
N_DOM = 4


def draw_sources(key, part):
    blocks = jnp.arange(NBLK)
    device = blocks // BLK_DEV
    place = blocks % BLK_DEV
    lowest = jnp.maximum(device * BLK_DEV - 1, 0)
    highest = jnp.minimum((device + 1) * BLK_DEV + 1, NBLK)
    picks = jax.random.randint(key, (NBLK, KNB), 0, 1 << 20)
    chosen = lowest[:, None] + picks % (highest - lowest)[:, None]
    left_edge = (place == 0) & (device > 0)
    right_edge = (place == BLK_DEV - 1) & (device < N_DOM - 1)
    second = jnp.where(left_edge, blocks - 1, jnp.where(right_edge, blocks + 1, chosen[:, 1]))
    chosen = chosen.at[:, 1].set(second).at[:, 0].set(blocks)
    return chosen.astype(jnp.int32)


def draw_counts(key, part):
    blocks = jnp.arange(NBLK)
    device = blocks // BLK_DEV
    place = blocks % BLK_DEV
    edge = (place == 0) & (device > 0) | (place == BLK_DEV - 1) & (device < N_DOM - 1)
    drawn = jax.random.randint(key, (NBLK,), 1, KNB + 1)
    drawn = jnp.where(edge, jnp.maximum(drawn, 2), drawn)
    drawn = drawn.at[0].set(1).at[NBLK - 1].set(KNB)
    return drawn.astype(jnp.int32)


def draw_tiles(key, part):
    base = jax.random.fold_in(key, 71)
    key_diag, key_back = jax.random.split(base)
    shape = (NBLK, KNB, BS, BS)
    diag = jax.random.uniform(key_diag, (NBLK, KNB, BS), jnp.float32, 0.4, 1.0)
    low = jnp.log(jnp.float32(0.0005))
    high = jnp.log(jnp.float32(0.005))
    back = jnp.exp(jax.random.uniform(key_back, shape, jnp.float32, 0.0, 1.0) * (high - low) + low)
    eye = jnp.arange(BS)[:, None] == jnp.arange(BS)[None, :]
    tiles = jnp.where(eye[None, None, :, :], diag[:, :, :, None], back)
    return tiles.astype(jnp.bfloat16)


def draw_cotangent(key, part):
    base = jax.random.fold_in(key, 83)
    shape = (MB, NODES, HID)
    values = jnp.clip(jax.random.normal(base, shape, jnp.float32), -3.0, 3.0)
    return values.astype(jnp.bfloat16)


def block_scale(rng, dims, pieces, smallest, largest):
    loudness = 1.0
    for axis_at, parts in pieces:
        steps = jax.random.uniform(jax.random.fold_in(jax.random.fold_in(rng, 6), axis_at), (parts,), jnp.float32, smallest / len(pieces), largest / len(pieces))
        loudness = loudness * jnp.repeat(jnp.exp(steps), dims[axis_at] // parts).reshape((-1,) + (1,) * (len(dims) - 1 - axis_at))
    return loudness


def bell_draw(key, dims, width, reach, cuts=(), held_as=jnp.bfloat16):
    result = width * jax.random.normal(key, dims, jnp.float32)
    if cuts:
        result = result * block_scale(key, dims, cuts, -0.22, 0.18)
    return jnp.clip(result, -reach, reach).astype(held_as)


def setup_inputs(seed: int = 0) -> dict:
    seeds = jax.random.split(jax.random.key(seed), 7)
    return {
        "features": bell_draw(seeds[0], (MB, NODES, HID), 1.0, 6.0, ((1, 4),)),
        "cotangent": draw_cotangent(jax.random.fold_in(seeds[6], 71), 0),
        "weights": bell_draw(seeds[2], (LAYERS, HID, HID), HID ** -0.5, 0.375, ((0, 8),)),
        "tiles": draw_tiles(jax.random.fold_in(seeds[6], 71), 0),
        "sources": draw_sources(jax.random.fold_in(seeds[6], 71), 0),
        "counts": draw_counts(jax.random.fold_in(seeds[6], 71), 0),
    }


epsilon = 1e-06

def reference(features, cotangent, weights, tiles, sources, counts):
    used = (jnp.arange(KNB)[None, :] < counts[:, None]).astype(jnp.bfloat16)
    masked = tiles * used[:, :, None, None]
    wide = masked.astype(jnp.float32)
    degree = lax.optimization_barrier(jnp.sum(wide, axis=(1, 3)))

    def aggregate(hidden):
        picked = hidden.reshape(NBLK, BS, HID)[sources].astype(jnp.float32)
        summed = jnp.einsum('bkij,bkjh->bih', wide, picked)
        return (summed / degree[:, :, None]).reshape(NODES, HID)

    def normalize(agg):
        scale = lax.rsqrt(lax.optimization_barrier(jnp.mean(agg * agg, axis=-1, keepdims=True)) + epsilon)
        return ((agg * scale).astype(jnp.bfloat16), scale)
    grads = [jnp.zeros((HID, HID), jnp.float32) for layer in range(LAYERS)]
    for snap in range(MB):
        hidden = features[snap]
        inputs = []
        for layer in range(LAYERS):
            inputs.append(hidden)
            agg = aggregate(hidden)
            nrm, scale = normalize(agg)
            z_val = jnp.dot(nrm, weights[layer], preferred_element_type=jnp.float32)
            hidden = (hidden.astype(jnp.float32) + jax.nn.silu(z_val)).astype(jnp.bfloat16)
        grad_bf = cotangent[snap]
        for layer in range(LAYERS - 1, -1, -1):
            agg = aggregate(inputs[layer])
            nrm, scale = normalize(agg)
            z_val = jnp.dot(nrm, weights[layer], preferred_element_type=jnp.float32)
            grad = grad_bf.astype(jnp.float32)
            sig = jax.nn.sigmoid(z_val)
            dz_val = (grad * sig * (1.0 + z_val * (1.0 - sig))).astype(jnp.bfloat16)
            grads[layer] = grads[layer] + jnp.dot(nrm.T, dz_val, preferred_element_type=jnp.float32)
            dnrm = jnp.dot(dz_val, weights[layer].T, preferred_element_type=jnp.float32)
            dagg = scale * (dnrm - agg * scale * scale * lax.optimization_barrier(jnp.mean(dnrm * agg, axis=-1, keepdims=True)))
            dsum = (dagg.reshape(NBLK, BS, HID) / degree[:, :, None]).astype(jnp.bfloat16)
            dpicked = jnp.einsum('bkij,bih->bkjh', wide, dsum.astype(jnp.float32))
            contrib = jnp.zeros((NBLK, BS, HID), jnp.float32).at[sources.reshape(-1)].add(dpicked.reshape(NBLK * KNB, BS, HID))
            grad_bf = (grad + contrib.reshape(NODES, HID)).astype(jnp.bfloat16)
    return jnp.stack(grads) * (1.0 / math.sqrt(MB * NODES))
```

```python
import functools
import math

import jax
import jax.numpy as jnp
from jax import lax
from jax.experimental import pallas as pl
from jax.experimental.pallas import tpu as pltpu
from jax.sharding import PartitionSpec as P

epsilon = 1e-06
BF = jnp.bfloat16
F32 = jnp.float32
BOTH = ("section", "dom")
NT = (((1,), (1,)), ((), ()))


def adjacency_kernel(place, sources, counts, tiles, dense, acc):
    nblk, width, bsize, _ = tiles.shape
    first = place[1] * nblk - 1
    acc[...] = jnp.zeros_like(acc)
    for b in range(nblk):
        rows = slice(b * bsize, (b + 1) * bsize)
        for k in range(width):
            used = (k < counts[b]).astype(F32)
            start = pl.multiple_of((sources[b, k] - first) * bsize, bsize)
            acc[rows, pl.ds(start, bsize)] += tiles[b, k].astype(F32) * used
    total = acc[...]
    dense[...] = (total / jnp.sum(total, axis=1, keepdims=True)).astype(BF)


def adjacency(place, tiles, sources, counts):
    nblk, width, bsize, _ = tiles.shape
    shape = (nblk * bsize, (nblk + 2) * bsize)
    smem = pl.BlockSpec(memory_space=pltpu.SMEM)
    return pl.pallas_call(
        adjacency_kernel,
        out_shape=jax.ShapeDtypeStruct(shape, BF),
        in_specs=[smem, smem, smem, pl.BlockSpec(memory_space=pltpu.VMEM)],
        out_specs=pl.BlockSpec(memory_space=pltpu.VMEM),
        scratch_shapes=[pltpu.VMEM(shape, F32)],
    )(place, sources, counts, tiles)


def step_kernel(doms, layers, bsize, *refs):
    place = refs[0]
    adj_in = refs[1 : 1 + doms]
    feat_in = refs[1 + doms : 1 + 2 * doms]
    cot_in = refs[1 + 2 * doms : 1 + 3 * doms]
    w_in = refs[1 + 3 * doms : 1 + 3 * doms + layers]
    (grads, adj, stage, weight, weight_t, hpad, nrm, slope, scale, dz, grad, sems) = refs[
        1 + 3 * doms + layers :
    ]
    section, dom = place[0], place[1]
    span = adj.shape[1]
    reach = adj.shape[2]
    feats = hpad.shape[1]
    nodes = doms * span

    def fill(pieces, target, lane):
        copies = []
        for j, piece in enumerate(pieces):
            at = lax.rem(dom + j, doms)
            copies.append(pltpu.make_async_copy(piece, target(at), sems.at[lane, j]))
        for copy in copies:
            copy.start()
        return copies

    w_copies = []
    for k in range(layers):
        slot = lax.rem(section + k, layers)
        w_copies.append(pltpu.make_async_copy(w_in[k], weight.at[slot], sems.at[3, k]))
    f_copies = fill(
        feat_in, lambda at: stage.at[0, pl.ds(pl.multiple_of(at * span, span), span)], 0
    )
    a_copies = fill(adj_in, lambda at: adj.at[at], 1)
    for copy in w_copies:
        copy.start()
    c_copies = fill(
        cot_in, lambda at: stage.at[1, pl.ds(pl.multiple_of(at * span, span), span)], 2
    )
    edge = jnp.zeros((feats, bsize), BF)
    for half in range(2):
        hpad[half, :, :bsize] = edge
        hpad[half, :, bsize + nodes :] = edge
    for copy in f_copies:
        copy.wait()
    hpad[0, :, bsize : bsize + nodes] = stage[0].T
    for copy in w_copies:
        copy.wait()
    for layer in range(layers):
        weight_t[layer] = weight[layer].T
    for copy in a_copies:
        copy.wait()

    def forward(layer, carry):
        now = lax.rem(layer, 2)
        later = 1 - now
        for d in range(doms):
            cols = slice(d * span, (d + 1) * span)
            own = slice(bsize + d * span, bsize + (d + 1) * span)
            agg = lax.dot_general(
                hpad[now, :, d * span : d * span + reach], adj[d], NT, preferred_element_type=F32
            )
            mean = jnp.sum(agg * agg, axis=0, keepdims=True) * (1.0 / feats)
            factor = lax.rsqrt(mean + epsilon)
            unit = (agg * factor).astype(BF)
            z_val = jnp.dot(weight_t[layer], unit, preferred_element_type=F32)
            sig = 0.5 * jnp.tanh(0.5 * z_val) + 0.5
            act = z_val * sig
            scale[layer, :, cols] = factor
            nrm[layer, :, cols] = unit
            slope[layer, :, cols] = (sig + act * (1.0 - sig)).astype(BF)
            hpad[later, :, own] = (hpad[now, :, own].astype(F32) + act).astype(BF)
        return carry

    lax.fori_loop(0, layers, forward, 0)

    for copy in c_copies:
        copy.wait()
    grad[:, bsize : bsize + nodes] = stage[1].astype(F32).T

    def weight_grad(layer):
        for d in range(doms):
            cols = slice(d * span, (d + 1) * span)
            own = slice(bsize + d * span, bsize + (d + 1) * span)
            dz[:, cols] = (grad[:, own] * slope[layer, :, cols].astype(F32)).astype(BF)
        dweight = lax.dot_general(nrm[layer], dz[...], NT, preferred_element_type=F32)
        grads[layer] = dweight.astype(BF)

    def backward(step, carry):
        layer = layers - 1 - step
        weight_grad(layer)
        for d in range(doms):
            cols = slice(d * span, (d + 1) * span)
            wide = slice(d * span, d * span + reach)
            dnrm = jnp.dot(weight[layer], dz[:, cols], preferred_element_type=F32)
            unit = nrm[layer, :, cols].astype(F32)
            mean = jnp.sum(dnrm * unit, axis=0, keepdims=True) * (1.0 / feats)
            dagg = (scale[layer, :, cols] * (dnrm - unit * mean)).astype(BF)
            grad[:, wide] += jnp.dot(dagg, adj[d], preferred_element_type=F32)
        return carry

    lax.fori_loop(0, layers - 1, backward, 0)
    weight_grad(0)


def train_step(place, adj_in, feat_in, cot_in, w_in, bsize):
    doms = len(adj_in)
    layers = len(w_in)
    span, reach = adj_in[0].shape
    feats = feat_in[0].shape[1]
    nodes = doms * span
    padded = nodes + 2 * bsize
    anywhere = pl.BlockSpec(memory_space=pl.ANY)
    return pl.pallas_call(
        functools.partial(step_kernel, doms, layers, bsize),
        out_shape=jax.ShapeDtypeStruct((layers, feats, feats), BF),
        in_specs=[pl.BlockSpec(memory_space=pltpu.SMEM)] + [anywhere] * (3 * doms + layers),
        out_specs=pl.BlockSpec(memory_space=pltpu.VMEM),
        scratch_shapes=[
            pltpu.VMEM((doms, span, reach), BF),
            pltpu.VMEM((2, nodes, feats), BF),
            pltpu.VMEM((layers, feats, feats), BF),
            pltpu.VMEM((layers, feats, feats), BF),
            pltpu.VMEM((2, feats, padded), BF),
            pltpu.VMEM((layers, feats, nodes), BF),
            pltpu.VMEM((layers, feats, nodes), BF),
            pltpu.VMEM((layers, 1, nodes), F32),
            pltpu.VMEM((feats, nodes), BF),
            pltpu.VMEM((feats, padded), F32),
            pltpu.SemaphoreType.DMA((4, max(doms, layers))),
        ],
        compiler_params=pltpu.CompilerParams(vmem_limit_bytes=60 * 2**20),
    )(place, *adj_in, *feat_in, *cot_in, *w_in)


def local(features, cotangent, weights, tiles, sources, counts):
    count, span, feats = features.shape
    bsize = tiles.shape[-1]
    sections = lax.axis_size("section")
    doms = lax.axis_size("dom")
    section = lax.axis_index("section")
    dom = lax.axis_index("dom")
    place = jnp.stack([section, dom]).astype(jnp.int32)
    half = doms // 2
    hosts = (count + 1) // 2

    def device(sec, rank):
        return sec * doms + rank

    homes = [(m // 2, (m % 2) * half) for m in range(count)]

    def pick(array, rank):
        snap = jnp.clip(2 * section + (rank >= half).astype(jnp.int32), 0, count - 1)
        return lax.dynamic_index_in_dim(array, snap, 0, False)

    def over_dom(make):
        pieces = [make(dom)]
        for j in range(1, doms):
            pairs = [(device(s, (a + j) % doms), device(s, a)) for s, a in homes]
            pieces.append(lax.ppermute(make(lax.rem(dom - j + doms, doms)), BOTH, pairs))
        return pieces

    feat_in = over_dom(lambda rank: pick(features, rank))
    dense = adjacency(place, tiles, sources, counts)
    adj_in = over_dom(lambda rank: dense)
    weight = weights[0]
    w_in = [weight]
    for k in range(1, sections):
        pairs = [(device((s + k) % sections, a), device(s, a)) for s, a in homes]
        w_in.append(lax.ppermute(weight, BOTH, pairs))
    cot_in = over_dom(lambda rank: pick(cotangent, rank))
    grads = train_step(place, adj_in, feat_in, cot_in, w_in, bsize)

    total = jnp.zeros((feats, feats), F32)
    for r in range(sections):
        pairs = []
        for s, a in homes:
            core = 0 if half < 2 else (2 * s) // hosts
            pairs.append((device(s, a), device((s + r) % sections, a + core)))
        piece = lax.dynamic_index_in_dim(grads, lax.rem(section + r, sections), 0, False)
        total = total + lax.ppermute(piece, BOTH, pairs).astype(F32)
    gathered = lax.all_gather(total.astype(BF), "dom")
    result = jnp.sum(gathered.astype(F32), axis=0) * (1.0 / math.sqrt(count * span * doms))
    return result[None]


def solution(mesh):
    in_specs = (
        P(None, "dom", None),
        P(None, "dom", None),
        P("section", None, None),
        P("dom", None, None, None),
        P("dom", None),
        P("dom"),
    )
    out_specs = P("section", None, None)
    return jax.shard_map(local, mesh=mesh, in_specs=in_specs, out_specs=out_specs, check_vma=False)
```

```python
import functools
import math

import jax
import jax.numpy as jnp
from jax import lax
from jax.experimental import pallas as pl
from jax.experimental.pallas import tpu as pltpu
from jax.sharding import PartitionSpec as P

epsilon = 1e-06
BF = jnp.bfloat16
F32 = jnp.float32
BOTH = ("section", "dom")
NT = (((1,), (1,)), ((), ()))


def pack_kernel(doms, place, sources, counts, tiles, features, cotangent, *refs):
    packs, (acc, dense, sems) = refs[:doms], refs[doms:]
    nblk, width, bsize, _ = tiles.shape
    section, dom = place[0], place[1]
    count, _, feats = features.shape
    reach = dense.shape[1]
    copies = []
    for j in range(doms):
        target = lax.rem(dom + doms - j, doms)
        snap = jnp.minimum(2 * section + (target >= doms // 2).astype(jnp.int32), count - 1)
        for i, array in enumerate((features, cotangent)):
            cols = pl.ds(reach + i * feats, feats)
            copies.append(
                pltpu.make_async_copy(array.at[snap], packs[j].at[:, cols], sems.at[i, j])
            )
    for copy in copies:
        copy.start()
    first = dom * nblk - 1
    acc[...] = jnp.zeros_like(acc)
    for b in range(nblk):
        rows = slice(b * bsize, (b + 1) * bsize)
        for k in range(width):
            used = (k < counts[b]).astype(F32)
            start = pl.multiple_of((sources[b, k] - first) * bsize, bsize)
            acc[rows, pl.ds(start, bsize)] += tiles[b, k].astype(F32) * used
    total = acc[...]
    dense[...] = (total / jnp.sum(total, axis=1, keepdims=True)).astype(BF)
    for j in range(doms):
        copy = pltpu.make_async_copy(dense, packs[j].at[:, pl.ds(0, reach)], sems.at[2, j])
        copy.start()
        copies.append(copy)
    for copy in copies:
        copy.wait()


def pack_inputs(place, tiles, sources, counts, features, cotangent, doms):
    nblk, width, bsize, _ = tiles.shape
    _, span, feats = features.shape
    reach = (nblk + 2) * bsize
    smem = pl.BlockSpec(memory_space=pltpu.SMEM)
    anywhere = pl.BlockSpec(memory_space=pl.ANY)
    return pl.pallas_call(
        functools.partial(pack_kernel, doms),
        out_shape=[jax.ShapeDtypeStruct((span, reach + 2 * feats), BF)] * doms,
        in_specs=[smem, smem, smem, pl.BlockSpec(memory_space=pltpu.VMEM), anywhere, anywhere],
        out_specs=[anywhere] * doms,
        scratch_shapes=[
            pltpu.VMEM((span, reach), F32),
            pltpu.VMEM((span, reach), BF),
            pltpu.SemaphoreType.DMA((3, doms)),
        ],
    )(place, sources, counts, tiles, features, cotangent)


def step_kernel(doms, layers, bsize, order, *refs):
    place = refs[0]
    packs = refs[1 : 1 + doms]
    blocks = refs[1 + doms : 1 + doms + len(order)]
    (grads, adj, stage, weight, weight_t, hpad, nrm, slope, scale, dz, grad, sems) = refs[
        1 + doms + len(order) :
    ]
    section, dom = place[0], place[1]
    span = adj.shape[1]
    reach = adj.shape[2]
    feats = hpad.shape[1]
    nodes = doms * span

    f_copies, a_copies, c_copies, w_copies = [], [], [], []
    for j, pack in enumerate(packs):
        at = lax.rem(dom + j, doms)
        rows = pl.ds(pl.multiple_of(at * span, span), span)
        feat = pack.at[:, pl.ds(reach, feats)]
        cot = pack.at[:, pl.ds(reach + feats, feats)]
        f_copies.append(pltpu.make_async_copy(feat, stage.at[0, rows], sems.at[0, j]))
        a_copies.append(
            pltpu.make_async_copy(pack.at[:, pl.ds(0, reach)], adj.at[at], sems.at[1, j])
        )
        c_copies.append(pltpu.make_async_copy(cot, stage.at[1, rows], sems.at[2, j]))
    count = 0
    for block, masks in zip(blocks, order):
        for i, mask in enumerate(masks):
            slot = lax.bitwise_xor(section, mask)
            w_copies.append(
                pltpu.make_async_copy(block.at[i], weight.at[slot], sems.at[3, count])
            )
            count += 1
    for copy in f_copies + w_copies + a_copies + c_copies:
        copy.start()
    edge = jnp.zeros((feats, bsize), BF)
    for half in range(2):
        hpad[half, :, :bsize] = edge
        hpad[half, :, bsize + nodes :] = edge
    for copy in f_copies:
        copy.wait()
    hpad[0, :, bsize : bsize + nodes] = stage[0].T
    for copy in w_copies:
        copy.wait()
    for layer in range(layers):
        weight_t[layer] = weight[layer].T
    for copy in a_copies:
        copy.wait()

    def forward(layer, carry):
        now = lax.rem(layer, 2)
        later = 1 - now
        for d in range(doms):
            cols = slice(d * span, (d + 1) * span)
            own = slice(bsize + d * span, bsize + (d + 1) * span)
            agg = lax.dot_general(
                hpad[now, :, d * span : d * span + reach], adj[d], NT, preferred_element_type=F32
            )
            mean = jnp.sum(agg * agg, axis=0, keepdims=True) * (1.0 / feats)
            factor = lax.rsqrt(mean + epsilon)
            unit = (agg * factor).astype(BF)
            z_val = jnp.dot(weight_t[layer], unit, preferred_element_type=F32)
            sig = 0.5 * jnp.tanh(0.5 * z_val) + 0.5
            act = z_val * sig
            scale[layer, :, cols] = factor
            nrm[layer, :, cols] = unit
            slope[layer, :, cols] = (sig + act * (1.0 - sig)).astype(BF)
            hpad[later, :, own] = (hpad[now, :, own].astype(F32) + act).astype(BF)
        return carry

    lax.fori_loop(0, layers, forward, 0)

    for copy in c_copies:
        copy.wait()
    grad[:, bsize : bsize + nodes] = stage[1].astype(F32).T

    def weight_grad(layer):
        for d in range(doms):
            cols = slice(d * span, (d + 1) * span)
            own = slice(bsize + d * span, bsize + (d + 1) * span)
            dz[:, cols] = (grad[:, own] * slope[layer, :, cols].astype(F32)).astype(BF)
        dweight = lax.dot_general(nrm[layer], dz[...], NT, preferred_element_type=F32)
        grads[layer] = dweight.astype(BF)

    def backward(step, carry):
        layer = layers - 1 - step
        weight_grad(layer)
        for d in range(doms):
            cols = slice(d * span, (d + 1) * span)
            wide = slice(d * span, d * span + reach)
            dnrm = jnp.dot(weight[layer], dz[:, cols], preferred_element_type=F32)
            unit = nrm[layer, :, cols].astype(F32)
            mean = jnp.sum(dnrm * unit, axis=0, keepdims=True) * (1.0 / feats)
            dagg = (scale[layer, :, cols] * (dnrm - unit * mean)).astype(BF)
            grad[:, wide] += jnp.dot(dagg, adj[d], preferred_element_type=F32)
        return carry

    lax.fori_loop(0, layers - 1, backward, 0)
    weight_grad(0)


def train_step(place, packs, blocks, order, bsize, feats):
    doms = len(packs)
    layers = sum(len(masks) for masks in order)
    span = packs[0].shape[0]
    reach = packs[0].shape[1] - 2 * feats
    nodes = doms * span
    padded = nodes + 2 * bsize
    anywhere = pl.BlockSpec(memory_space=pl.ANY)
    return pl.pallas_call(
        functools.partial(step_kernel, doms, layers, bsize, order),
        out_shape=jax.ShapeDtypeStruct((layers, feats, feats), BF),
        in_specs=[pl.BlockSpec(memory_space=pltpu.SMEM)] + [anywhere] * (doms + len(blocks)),
        out_specs=pl.BlockSpec(memory_space=pltpu.VMEM),
        scratch_shapes=[
            pltpu.VMEM((doms, span, reach), BF),
            pltpu.VMEM((2, nodes, feats), BF),
            pltpu.VMEM((layers, feats, feats), BF),
            pltpu.VMEM((layers, feats, feats), BF),
            pltpu.VMEM((2, feats, padded), BF),
            pltpu.VMEM((layers, feats, nodes), BF),
            pltpu.VMEM((layers, feats, nodes), BF),
            pltpu.VMEM((layers, 1, nodes), F32),
            pltpu.VMEM((feats, nodes), BF),
            pltpu.VMEM((feats, padded), F32),
            pltpu.SemaphoreType.DMA((4, max(doms, layers))),
        ],
        compiler_params=pltpu.CompilerParams(vmem_limit_bytes=60 * 2**20),
    )(place, *packs, *blocks)


def local(features, cotangent, weights, tiles, sources, counts):
    count, span, feats = features.shape
    bsize = tiles.shape[-1]
    sections = lax.axis_size("section")
    doms = lax.axis_size("dom")
    section = lax.axis_index("section")
    dom = lax.axis_index("dom")
    place = jnp.stack([section, dom]).astype(jnp.int32)
    half = doms // 2
    hosts = (count + 1) // 2

    def device(sec, rank):
        return sec * doms + rank

    homes = [(m // 2, (m % 2) * half) for m in range(count)]

    blocks = [weights]
    order = [(0,)]
    mask = sections // 2
    while mask:
        pairs = [(device(s, a), device(s ^ mask, a)) for s in range(sections) for a in (0, half)]
        fresh = [lax.ppermute(block, BOTH, pairs) for block in blocks]
        flipped = [tuple(m ^ mask for m in masks) for masks in order]
        if mask == sections // 2:
            blocks = [jnp.concatenate(blocks + fresh, axis=0)]
            order = [order[0] + flipped[0]]
        else:
            blocks = blocks + fresh
            order = order + flipped
        mask //= 2

    packs = list(pack_inputs(place, tiles, sources, counts, features, cotangent, doms))
    for j in range(1, doms):
        pairs = [(device(s, (a + j) % doms), device(s, a)) for s, a in homes]
        packs[j] = lax.ppermute(packs[j], BOTH, pairs)
    grads = train_step(place, packs, blocks, tuple(order), bsize, feats)

    total = jnp.zeros((feats, feats), F32)
    for r in range(sections):
        pairs = []
        for s, a in homes:
            core = 0 if half < 2 else (2 * s) // hosts
            pairs.append((device(s, a), device((s + r) % sections, a + core)))
        piece = lax.dynamic_index_in_dim(grads, lax.rem(section + r, sections), 0, False)
        total = total + lax.ppermute(piece, BOTH, pairs).astype(F32)
    gathered = lax.all_gather(total.astype(BF), "dom")
    result = jnp.sum(gathered.astype(F32), axis=0) * (1.0 / math.sqrt(count * span * doms))
    return result[None]


def solution(mesh):
    in_specs = (
        P(None, "dom", None),
        P(None, "dom", None),
        P("section", None, None),
        P("dom", None, None, None),
        P("dom", None),
        P("dom"),
    )
    out_specs = P("section", None, None)
    return jax.shard_map(local, mesh=mesh, in_specs=in_specs, out_specs=out_specs, check_vma=False)
```

```python
import functools
import math

import jax
import jax.numpy as jnp
from jax import lax
from jax.experimental import pallas as pl
from jax.experimental.pallas import tpu as pltpu
from jax.sharding import PartitionSpec as P

epsilon = 1e-06
BF = jnp.bfloat16
F32 = jnp.float32
BOTH = ("section", "dom")
NT = (((1,), (1,)), ((), ()))


def pack_kernel(doms, place, sources, counts, tiles, features, cotangent, *refs):
    packs, (acc, dense, stage, sems) = refs[:doms], refs[doms:]
    nblk, width, bsize, _ = tiles.shape
    section, dom = place[0], place[1]
    count, _, feats = features.shape
    reach = dense.shape[1]
    reads, writes = [], []
    for j in range(doms):
        target = lax.rem(dom + doms - j, doms)
        snap = jnp.minimum(2 * section + (target >= doms // 2).astype(jnp.int32), count - 1)
        for i, array in enumerate((features, cotangent)):
            cols = pl.ds(i * feats, feats)
            reads.append(
                pltpu.make_async_copy(array.at[snap], stage.at[j, :, cols], sems.at[i, j])
            )
        writes.append(
            pltpu.make_async_copy(
                stage.at[j], packs[j].at[:, pl.ds(reach, 2 * feats)], sems.at[2, j]
            )
        )
    for copy in reads:
        copy.start()
    first = dom * nblk - 1
    acc[...] = jnp.zeros_like(acc)
    for b in range(nblk):
        rows = slice(b * bsize, (b + 1) * bsize)
        for k in range(width):
            used = (k < counts[b]).astype(F32)
            start = pl.multiple_of((sources[b, k] - first) * bsize, bsize)
            acc[rows, pl.ds(start, bsize)] += tiles[b, k].astype(F32) * used
    total = acc[...]
    dense[...] = (total / jnp.sum(total, axis=1, keepdims=True)).astype(BF)
    for j in range(doms):
        copy = pltpu.make_async_copy(dense, packs[j].at[:, pl.ds(0, reach)], sems.at[3, j])
        copy.start()
        writes.append(copy)
    for copy in reads:
        copy.wait()
    for copy in writes[:doms]:
        copy.start()
    for copy in writes:
        copy.wait()


def pack_inputs(place, tiles, sources, counts, features, cotangent, doms):
    nblk, width, bsize, _ = tiles.shape
    _, span, feats = features.shape
    reach = (nblk + 2) * bsize
    smem = pl.BlockSpec(memory_space=pltpu.SMEM)
    anywhere = pl.BlockSpec(memory_space=pl.ANY)
    return pl.pallas_call(
        functools.partial(pack_kernel, doms),
        out_shape=[jax.ShapeDtypeStruct((span, reach + 2 * feats), BF)] * doms,
        in_specs=[smem, smem, smem, pl.BlockSpec(memory_space=pltpu.VMEM), anywhere, anywhere],
        out_specs=[pl.BlockSpec(memory_space=pltpu.HBM)] * doms,
        scratch_shapes=[
            pltpu.VMEM((span, reach), F32),
            pltpu.VMEM((span, reach), BF),
            pltpu.VMEM((doms, span, 2 * feats), BF),
            pltpu.SemaphoreType.DMA((4, doms)),
        ],
    )(place, sources, counts, tiles, features, cotangent)


def step_kernel(doms, layers, bsize, order, *refs):
    place = refs[0]
    packs = refs[1 : 1 + doms]
    blocks = refs[1 + doms : 1 + doms + len(order)]
    (grads, adj, stage, weight, h_even, h_odd, nrm, slope, scale, dz, grad, sems) = refs[
        1 + doms + len(order) :
    ]
    section, dom = place[0], place[1]
    span = adj.shape[1]
    reach = adj.shape[2]
    feats = h_even.shape[0]
    nodes = doms * span

    f_copies, a_copies, c_copies, w_copies = [], [], [], []
    for j, pack in enumerate(packs):
        at = lax.rem(dom + j, doms)
        rows = pl.ds(pl.multiple_of(at * span, span), span)
        feat = pack.at[:, pl.ds(reach, feats)]
        cot = pack.at[:, pl.ds(reach + feats, feats)]
        f_copies.append(pltpu.make_async_copy(feat, stage.at[0, rows], sems.at[0, j]))
        a_copies.append(
            pltpu.make_async_copy(pack.at[:, pl.ds(0, reach)], adj.at[at], sems.at[1, j])
        )
        c_copies.append(pltpu.make_async_copy(cot, stage.at[1, rows], sems.at[2, j]))
    count = 0
    for block, masks in zip(blocks, order):
        for i, mask in enumerate(masks):
            slot = lax.bitwise_xor(section, mask)
            w_copies.append(
                pltpu.make_async_copy(block.at[i], weight.at[slot], sems.at[3, count])
            )
            count += 1
    for copy in f_copies + w_copies + a_copies + c_copies:
        copy.start()
    edge = jnp.zeros((feats, bsize), BF)
    for hidden in (h_even, h_odd):
        hidden[:, :bsize] = edge
        hidden[:, bsize + nodes :] = edge
    for copy in f_copies:
        copy.wait()
    h_even[:, bsize : bsize + nodes] = stage[0].T
    for copy in w_copies:
        copy.wait()
    for copy in a_copies:
        copy.wait()

    def forward_layers(base, size):
        steps = [(i, d) for i in range(size) for d in range(doms)]
        aggs, units, zvals, wts = {}, {}, {}, {}

        def bound(i):
            return (h_odd, h_even) if i % 2 else (h_even, h_odd)

        def gather(t):
            i, d = steps[t]
            src, _ = bound(i)
            aggs[t] = lax.dot_general(
                src[:, d * span : d * span + reach], adj[d], NT, preferred_element_type=F32
            )

        def project(t):
            i, d = steps[t]
            cols = slice(d * span, (d + 1) * span)
            agg = aggs.pop(t)
            mean = jnp.sum(agg * agg, axis=0, keepdims=True) * (1.0 / feats)
            factor = lax.rsqrt(mean + epsilon)
            unit = (agg * factor).astype(BF)
            scale[base + i, :, cols] = factor
            nrm[base + i, :, cols] = unit
            if d == 0:
                wts[i] = weight[base + i].T
            zvals[t] = jnp.dot(wts[i], unit, preferred_element_type=F32)

        def activate(t):
            i, d = steps[t]
            src, dst = bound(i)
            cols = slice(d * span, (d + 1) * span)
            own = slice(bsize + d * span, bsize + (d + 1) * span)
            z_val = zvals.pop(t)
            sig = 0.5 * jnp.tanh(0.5 * z_val) + 0.5
            act = z_val * sig
            slope[base + i, :, cols] = (sig + act * (1.0 - sig)).astype(BF)
            dst[:, own] = (src[:, own].astype(F32) + act).astype(BF)

        for t in range(len(steps) + 2):
            if 0 <= t - 2:
                activate(t - 2)
            if t < len(steps):
                gather(t)
            if 0 <= t - 1 < len(steps):
                project(t - 1)

    def backward_layers(top, size, last):
        steps = [(i, d) for i in range(size) for d in range(doms)]
        dnrms, spreads = {}, {}

        def begin(t):
            i, d = steps[t]
            cols = slice(d * span, (d + 1) * span)
            value = (grad[:, cols] * slope[top - i, :, cols].astype(F32)).astype(BF)
            dz[i % 2, :, cols] = value
            if not (last and i == size - 1):
                dnrms[t] = jnp.dot(weight[top - i], value, preferred_element_type=F32)

        def spread(t):
            i, d = steps[t]
            cols = slice(d * span, (d + 1) * span)
            dnrm = dnrms.pop(t)
            unit = nrm[top - i, :, cols].astype(F32)
            mean = jnp.sum(dnrm * unit, axis=0, keepdims=True) * (1.0 / feats)
            dagg = (scale[top - i, :, cols] * (dnrm - unit * mean)).astype(BF)
            spreads[t] = jnp.dot(dagg, adj[d], preferred_element_type=F32)

        def update(t):
            i, d = steps[t]
            mine = spreads[t]
            low = mine[:, bsize : 2 * bsize]
            high = mine[:, span : span + bsize]
            if d > 0:
                low = low + spreads.pop(t - 1)[:, span + bsize :]
            if d < doms - 1:
                high = high + spreads[t + 1][:, :bsize]
            at = d * span
            grad[:, at : at + bsize] += low
            if span > 2 * bsize:
                grad[:, at + bsize : at + span - bsize] += mine[:, 2 * bsize : span]
            grad[:, at + span - bsize : at + span] += high

        def weigh(i):
            dweight = lax.dot_general(nrm[top - i], dz[i % 2], NT, preferred_element_type=F32)
            grads[top - i] = dweight.astype(BF)

        full = len(steps) - (doms if last else 0)
        for t in range(len(steps) + 2):
            if t and t % doms == 0 and t <= len(steps):
                weigh(t // doms - 1)
            if t < len(steps):
                begin(t)
            if 0 <= t - 1 < full:
                spread(t - 1)
            if 0 <= t - 2 < full:
                update(t - 2)

    small = layers * doms <= 32
    if small:
        forward_layers(0, layers)
    else:
        lax.fori_loop(0, layers // 2, lambda p, c: (forward_layers(2 * p, 2), c)[1], 0)
        if layers % 2:
            forward_layers(layers - 1, 1)

    for copy in c_copies:
        copy.wait()
    grad[...] = stage[1].astype(F32).T

    if small:
        backward_layers(layers - 1, layers, True)
    else:
        lax.fori_loop(
            0, layers - 1, lambda p, c: (backward_layers(layers - 1 - p, 1, False), c)[1], 0
        )
        backward_layers(0, 1, True)


def train_step(place, packs, blocks, order, bsize, feats):
    doms = len(packs)
    layers = sum(len(masks) for masks in order)
    span = packs[0].shape[0]
    reach = packs[0].shape[1] - 2 * feats
    nodes = doms * span
    padded = nodes + 2 * bsize
    anywhere = pl.BlockSpec(memory_space=pl.ANY)
    return pl.pallas_call(
        functools.partial(step_kernel, doms, layers, bsize, order),
        out_shape=jax.ShapeDtypeStruct((layers, feats, feats), BF),
        in_specs=[pl.BlockSpec(memory_space=pltpu.SMEM)] + [anywhere] * (doms + len(blocks)),
        out_specs=pl.BlockSpec(memory_space=pltpu.VMEM),
        scratch_shapes=[
            pltpu.VMEM((doms, span, reach), BF),
            pltpu.VMEM((2, nodes, feats), BF),
            pltpu.VMEM((layers, feats, feats), BF),
            pltpu.VMEM((feats, padded), BF),
            pltpu.VMEM((feats, padded), BF),
            pltpu.VMEM((layers, feats, nodes), BF),
            pltpu.VMEM((layers, feats, nodes), BF),
            pltpu.VMEM((layers, 1, nodes), F32),
            pltpu.VMEM((2, feats, nodes), BF),
            pltpu.VMEM((feats, nodes), F32),
            pltpu.SemaphoreType.DMA((4, max(doms, layers))),
        ],
        compiler_params=pltpu.CompilerParams(vmem_limit_bytes=60 * 2**20),
    )(place, *packs, *blocks)


def local(features, cotangent, weights, tiles, sources, counts):
    count, span, feats = features.shape
    bsize = tiles.shape[-1]
    sections = lax.axis_size("section")
    doms = lax.axis_size("dom")
    section = lax.axis_index("section")
    dom = lax.axis_index("dom")
    place = jnp.stack([section, dom]).astype(jnp.int32)
    half = doms // 2
    hosts = (count + 1) // 2

    def device(sec, rank):
        return sec * doms + rank

    homes = [(m // 2, (m % 2) * half) for m in range(count)]

    blocks = [weights]
    order = [(0,)]
    mask = sections // 2
    while mask:
        pairs = [(device(s, a), device(s ^ mask, a)) for s in range(sections) for a in (0, half)]
        fresh = [lax.ppermute(block, BOTH, pairs) for block in blocks]
        flipped = [tuple(m ^ mask for m in masks) for masks in order]
        if mask == sections // 2:
            blocks = [jnp.concatenate(blocks + fresh, axis=0)]
            order = [order[0] + flipped[0]]
        else:
            blocks = blocks + fresh
            order = order + flipped
        mask //= 2

    packs = list(pack_inputs(place, tiles, sources, counts, features, cotangent, doms))
    for j in range(1, doms):
        pairs = [(device(s, (a + j) % doms), device(s, a)) for s, a in homes]
        packs[j] = lax.ppermute(packs[j], BOTH, pairs)
    grads = train_step(place, packs, blocks, tuple(order), bsize, feats)

    total = jnp.zeros((feats, feats), F32)
    for r in range(sections):
        pairs = []
        for s, a in homes:
            core = 0 if half < 2 else (2 * s) // hosts
            pairs.append((device(s, a), device((s + r) % sections, a + core)))
        piece = lax.dynamic_index_in_dim(grads, lax.rem(section + r, sections), 0, False)
        total = total + lax.ppermute(piece, BOTH, pairs).astype(F32)
    gathered = lax.all_gather(total.astype(BF), "dom")
    result = jnp.sum(gathered.astype(F32), axis=0) * (1.0 / math.sqrt(count * span * doms))
    return result[None]


def solution(mesh):
    in_specs = (
        P(None, "dom", None),
        P(None, "dom", None),
        P("section", None, None),
        P("dom", None, None, None),
        P("dom", None),
        P("dom"),
    )
    out_specs = P("section", None, None)
    return jax.shard_map(local, mesh=mesh, in_specs=in_specs, out_specs=out_specs, check_vma=False)
```

```python
import functools
import math

import jax
import jax.numpy as jnp
from jax import lax
from jax.experimental import pallas as pl
from jax.experimental.pallas import tpu as pltpu
from jax.sharding import PartitionSpec as P

epsilon = 1e-06
BF = jnp.bfloat16
F32 = jnp.float32
BOTH = ("section", "dom")
NT = (((1,), (1,)), ((), ()))


def pack_kernel(doms, place, sources, counts, tiles, features, cotangent, *refs):
    chips = doms // 2
    packs, (acc, dense, stage, sems) = refs[:chips], refs[chips:]
    nblk, width, bsize, _ = tiles.shape
    section, dom = place[0], place[1]
    count, _, feats = features.shape
    reach = dense.shape[1]
    reads, writes = [], []
    for j in range(chips):
        target = lax.rem(dom + doms - 2 * j, doms)
        snap = jnp.minimum(2 * section + (target >= doms // 2).astype(jnp.int32), count - 1)
        for i, array in enumerate((features, cotangent)):
            cols = pl.ds(i * feats, feats)
            reads.append(
                pltpu.make_async_copy(array.at[snap], stage.at[j, :, cols], sems.at[i, j])
            )
        writes.append(
            pltpu.make_async_copy(
                stage.at[j], packs[j].at[:, pl.ds(reach, 2 * feats)], sems.at[2, j]
            )
        )
    for copy in reads:
        copy.start()
    first = dom * nblk - 1
    acc[...] = jnp.zeros_like(acc)
    for b in range(nblk):
        rows = slice(b * bsize, (b + 1) * bsize)
        for k in range(width):
            used = (k < counts[b]).astype(F32)
            start = pl.multiple_of((sources[b, k] - first) * bsize, bsize)
            acc[rows, pl.ds(start, bsize)] += tiles[b, k].astype(F32) * used
    total = acc[...]
    dense[...] = (total / jnp.sum(total, axis=1, keepdims=True)).astype(BF)
    for j in range(chips):
        copy = pltpu.make_async_copy(dense, packs[j].at[:, pl.ds(0, reach)], sems.at[3, j])
        copy.start()
        writes.append(copy)
    for copy in reads:
        copy.wait()
    for copy in writes[:chips]:
        copy.start()
    for copy in writes:
        copy.wait()


def pack_inputs(place, tiles, sources, counts, features, cotangent, doms):
    nblk, width, bsize, _ = tiles.shape
    _, span, feats = features.shape
    reach = (nblk + 2) * bsize
    chips = doms // 2
    smem = pl.BlockSpec(memory_space=pltpu.SMEM)
    anywhere = pl.BlockSpec(memory_space=pl.ANY)
    return pl.pallas_call(
        functools.partial(pack_kernel, doms),
        out_shape=[jax.ShapeDtypeStruct((span, reach + 2 * feats), BF)] * chips,
        in_specs=[smem, smem, smem, pl.BlockSpec(memory_space=pltpu.VMEM), anywhere, anywhere],
        out_specs=[pl.BlockSpec(memory_space=pltpu.HBM)] * chips,
        scratch_shapes=[
            pltpu.VMEM((span, reach), F32),
            pltpu.VMEM((span, reach), BF),
            pltpu.VMEM((chips, span, 2 * feats), BF),
            pltpu.SemaphoreType.DMA((4, chips)),
        ],
    )(place, sources, counts, tiles, features, cotangent)


def step_kernel(doms, layers, count, bsize, order, *refs):
    place = refs[0]
    packs = refs[1 : 1 + doms]
    blocks = refs[1 + doms : 1 + doms + 2 * len(order)]
    (keep, give, adj, stage, weight, h_even, h_odd, nrm, slope, scale, dz, grad, sems) = refs[
        1 + doms + 2 * len(order) :
    ]
    section, dom = place[0], place[1]
    span = adj.shape[1]
    reach = adj.shape[2]
    feats = h_even.shape[0]
    nodes = doms * span
    half = doms // 2
    late = (dom >= half).astype(jnp.int32)
    active = (lax.rem(dom, half) == 0) & (2 * section + late < count)

    @pl.when(jnp.logical_not(active))
    def _():
        keep[...] = jnp.zeros_like(keep)
        give[...] = jnp.zeros_like(give)

    @pl.when(active)
    def _():
        f_copies, a_copies, c_copies, w_copies = [], [], [], []
        for j, pack in enumerate(packs):
            start = dom if j < half else lax.bitwise_xor(dom, 1)
            at = lax.rem(start + 2 * lax.rem(j, half), doms)
            rows = pl.ds(pl.multiple_of(at * span, span), span)
            feat = pack.at[:, pl.ds(reach, feats)]
            cot = pack.at[:, pl.ds(reach + feats, feats)]
            f_copies.append(pltpu.make_async_copy(feat, stage.at[0, rows], sems.at[0, j]))
            a_copies.append(
                pltpu.make_async_copy(pack.at[:, pl.ds(0, reach)], adj.at[at], sems.at[1, j])
            )
            c_copies.append(pltpu.make_async_copy(cot, stage.at[1, rows], sems.at[2, j]))
        for side in range(2):
            rows = pl.ds(side * (feats // 2), feats // 2)
            index = 0
            for block, masks in zip(blocks[side * len(order) :], order):
                for i, mask in enumerate(masks):
                    slot = lax.bitwise_xor(section, mask)
                    w_copies.append(
                        pltpu.make_async_copy(
                            block.at[i], weight.at[slot, rows], sems.at[3 + side, index]
                        )
                    )
                    index += 1
        for copy in f_copies + w_copies + a_copies + c_copies:
            copy.start()
        edge = jnp.zeros((feats, bsize), BF)
        for hidden in (h_even, h_odd):
            hidden[:, :bsize] = edge
            hidden[:, bsize + nodes :] = edge
        for copy in f_copies:
            copy.wait()
        h_even[:, bsize : bsize + nodes] = stage[0].T
        for copy in w_copies:
            copy.wait()
        for copy in a_copies:
            copy.wait()

        def forward_layers(base, size):
            steps = [(i, d) for i in range(size) for d in range(doms)]
            aggs, units, zvals, wts = {}, {}, {}, {}

            def bound(i):
                return (h_odd, h_even) if i % 2 else (h_even, h_odd)

            def gather(t):
                i, d = steps[t]
                src, _ = bound(i)
                aggs[t] = lax.dot_general(
                    src[:, d * span : d * span + reach], adj[d], NT, preferred_element_type=F32
                )

            def project(t):
                i, d = steps[t]
                cols = slice(d * span, (d + 1) * span)
                agg = aggs.pop(t)
                mean = jnp.sum(agg * agg, axis=0, keepdims=True) * (1.0 / feats)
                factor = lax.rsqrt(mean + epsilon)
                unit = (agg * factor).astype(BF)
                scale[base + i, :, cols] = factor
                nrm[base + i, :, cols] = unit
                if d == 0:
                    wts[i] = weight[base + i].T
                zvals[t] = jnp.dot(wts[i], unit, preferred_element_type=F32)

            def activate(t):
                i, d = steps[t]
                src, dst = bound(i)
                cols = slice(d * span, (d + 1) * span)
                own = slice(bsize + d * span, bsize + (d + 1) * span)
                z_val = zvals.pop(t)
                sig = 0.5 * jnp.tanh(0.5 * z_val) + 0.5
                act = z_val * sig
                slope[base + i, :, cols] = (sig + act * (1.0 - sig)).astype(BF)
                dst[:, own] = (src[:, own].astype(F32) + act).astype(BF)

            for t in range(len(steps) + 2):
                if 0 <= t - 2:
                    activate(t - 2)
                if t < len(steps):
                    gather(t)
                if 0 <= t - 1 < len(steps):
                    project(t - 1)

        def backward_layers(top, size, last):
            steps = [(i, d) for i in range(size) for d in range(doms)]
            dnrms, spreads = {}, {}

            def begin(t):
                i, d = steps[t]
                cols = slice(d * span, (d + 1) * span)
                value = (grad[:, cols] * slope[top - i, :, cols].astype(F32)).astype(BF)
                dz[i % 2, :, cols] = value
                if not (last and i == size - 1):
                    dnrms[t] = jnp.dot(weight[top - i], value, preferred_element_type=F32)

            def spread(t):
                i, d = steps[t]
                cols = slice(d * span, (d + 1) * span)
                dnrm = dnrms.pop(t)
                unit = nrm[top - i, :, cols].astype(F32)
                mean = jnp.sum(dnrm * unit, axis=0, keepdims=True) * (1.0 / feats)
                dagg = (scale[top - i, :, cols] * (dnrm - unit * mean)).astype(BF)
                spreads[t] = jnp.dot(dagg, adj[d], preferred_element_type=F32)

            def update(t):
                i, d = steps[t]
                mine = spreads[t]
                low = mine[:, bsize : 2 * bsize]
                high = mine[:, span : span + bsize]
                if d > 0:
                    low = low + spreads.pop(t - 1)[:, span + bsize :]
                if d < doms - 1:
                    high = high + spreads[t + 1][:, :bsize]
                at = d * span
                grad[:, at : at + bsize] += low
                if span > 2 * bsize:
                    grad[:, at + bsize : at + span - bsize] += mine[:, 2 * bsize : span]
                grad[:, at + span - bsize : at + span] += high

            def weigh(i):
                dweight = lax.dot_general(nrm[top - i], dz[i % 2], NT, preferred_element_type=F32)
                keep[top - i] = dweight[: feats // 2].astype(BF)
                give[top - i] = dweight[feats // 2 :].astype(BF)

            full = len(steps) - (doms if last else 0)
            for t in range(len(steps) + 2):
                if t and t % doms == 0 and t <= len(steps):
                    weigh(t // doms - 1)
                if t < len(steps):
                    begin(t)
                if 0 <= t - 1 < full:
                    spread(t - 1)
                if 0 <= t - 2 < full:
                    update(t - 2)

        small = layers * doms <= 32
        if small:
            forward_layers(0, layers)
        else:
            lax.fori_loop(0, layers // 2, lambda p, c: (forward_layers(2 * p, 2), c)[1], 0)
            if layers % 2:
                forward_layers(layers - 1, 1)

        for copy in c_copies:
            copy.wait()
        grad[...] = stage[1].astype(F32).T

        if small:
            backward_layers(layers - 1, layers, True)
        else:
            lax.fori_loop(
                0, layers - 1, lambda p, c: (backward_layers(layers - 1 - p, 1, False), c)[1], 0
            )
            backward_layers(0, 1, True)


def train_step(place, packs, blocks, order, count, bsize, feats):
    doms = len(packs)
    layers = sum(len(masks) for masks in order)
    span = packs[0].shape[0]
    reach = packs[0].shape[1] - 2 * feats
    nodes = doms * span
    padded = nodes + 2 * bsize
    anywhere = pl.BlockSpec(memory_space=pl.ANY)
    need = layers * feats * (4 * nodes + 32 * nodes // feats + 6 * feats) + 16 * 2**20
    need = min(need, 60 * 2**20)
    return pl.pallas_call(
        functools.partial(step_kernel, doms, layers, count, bsize, order),
        out_shape=[jax.ShapeDtypeStruct((layers, feats // 2, feats), BF)] * 2,
        in_specs=[
            pl.BlockSpec(memory_space=pltpu.SMEM),
            pl.BlockSpec(memory_space=pltpu.HBM),
        ]
        + [anywhere] * (doms - 1 + len(blocks)),
        out_specs=[pl.BlockSpec(memory_space=pltpu.VMEM)] * 2,
        scratch_shapes=[
            pltpu.VMEM((doms, span, reach), BF),
            pltpu.VMEM((2, nodes, feats), BF),
            pltpu.VMEM((layers, feats, feats), BF),
            pltpu.VMEM((feats, padded), BF),
            pltpu.VMEM((feats, padded), BF),
            pltpu.VMEM((layers, feats, nodes), BF),
            pltpu.VMEM((layers, feats, nodes), BF),
            pltpu.VMEM((layers, 1, nodes), F32),
            pltpu.VMEM((2, feats, nodes), BF),
            pltpu.VMEM((feats, nodes), F32),
            pltpu.SemaphoreType.DMA((5, max(doms, layers))),
        ],
        compiler_params=pltpu.CompilerParams(vmem_limit_bytes=need),
    )(place, *packs, *blocks)


def local(features, cotangent, weights, tiles, sources, counts):
    count, span, feats = features.shape
    bsize = tiles.shape[-1]
    sections = lax.axis_size("section")
    doms = lax.axis_size("dom")
    section = lax.axis_index("section")
    dom = lax.axis_index("dom")
    core = lax.rem(dom, 2)
    place = jnp.stack([section, dom]).astype(jnp.int32)
    rows = feats // 2

    def move(array, where):
        pairs = []
        for s in range(sections):
            for d in range(doms):
                to_s, to_d = where(s, d)
                pairs.append((s * doms + d, to_s * doms + to_d))
        return lax.ppermute(array, BOTH, pairs)

    def swap_core(array):
        return move(array, lambda s, d: (s, d ^ 1))

    def swap_section(array, mask):
        return move(array, lambda s, d: (s ^ mask, d))

    def shift_chip(array, by):
        return move(array, lambda s, d: (s, (d - 2 * by) % doms))

    packs = list(pack_inputs(place, tiles, sources, counts, features, cotangent, doms))
    packs = packs[:1] + [shift_chip(pack, j) for j, pack in enumerate(packs) if j]
    near = swap_core(packs[0])

    blocks = [lax.dynamic_slice_in_dim(weights, core * rows, rows, 1)]
    order = [(0,)]
    mask = sections // 2
    while mask:
        fresh = [swap_section(block, mask) for block in blocks]
        flipped = [tuple(m ^ mask for m in masks) for masks in order]
        if mask == sections // 2:
            blocks = [jnp.concatenate(blocks + fresh, axis=0)]
            order = [order[0] + flipped[0]]
        else:
            blocks = blocks + fresh
            order = order + flipped
        mask //= 2
    far, blocks = lax.optimization_barrier((packs[1:], blocks))
    packs = packs[:1] + far + [near] + [swap_core(pack) for pack in far]
    blocks = blocks + [swap_core(block) for block in blocks]
    keep, give = train_step(place, packs, blocks, tuple(order), count, bsize, feats)

    halves = keep + swap_core(give)
    total = lax.dynamic_index_in_dim(halves, section, 0, False).astype(F32)
    for mask in reversed(range(1, sections)):
        piece = lax.dynamic_index_in_dim(halves, lax.bitwise_xor(section, mask), 0, False)
        total = total + swap_section(piece, mask).astype(F32)
    part = total.astype(BF)
    parts = [part] + [shift_chip(part, j) for j in range(1, doms // 2)]
    if len(parts) > 2:
        ring = jnp.stack(parts)
        parts = [
            lax.dynamic_index_in_dim(ring, lax.rem(i - dom // 2 + len(parts), len(parts)), 0, False)
            for i in range(len(parts))
        ]
    total = sum(item.astype(F32) for item in parts)
    total = total * (1.0 / math.sqrt(count * span * doms))
    other = swap_core(total)
    first = jnp.where(core == 0, total, other)
    second = jnp.where(core == 0, other, total)
    return jnp.concatenate([first, second], axis=0)[None]


def solution(mesh):
    in_specs = (
        P(None, "dom", None),
        P(None, "dom", None),
        P("section", None, None),
        P("dom", None, None, None),
        P("dom", None),
        P("dom"),
    )
    out_specs = P("section", None, None)
    return jax.shard_map(local, mesh=mesh, in_specs=in_specs, out_specs=out_specs, check_vma=False)
```

```python
import functools
import math

import jax
import jax.numpy as jnp
from jax import lax
from jax.experimental import pallas as pl
from jax.experimental.pallas import tpu as pltpu
from jax.sharding import PartitionSpec as P

epsilon = 1e-06
BF = jnp.bfloat16
F32 = jnp.float32
BOTH = ("section", "dom")
NT = (((1,), (1,)), ((), ()))


def pack_kernel(doms, sources, counts, tiles, features, cotangent, *refs):
    chips = doms // 2
    packs, (acc, sems) = refs[:chips], refs[chips:]
    nblk, width, bsize, _ = tiles.shape
    section, dom = lax.axis_index("section"), lax.axis_index("dom")
    count, _, feats = features.shape
    reach = acc.shape[1]
    copies = []
    for j in range(chips):
        target = lax.rem(dom + doms - 2 * j, doms)
        snap = jnp.minimum(2 * section + (target >= doms // 2).astype(jnp.int32), count - 1)
        for i, array in enumerate((features, cotangent)):
            cols = pl.ds(reach + i * feats, feats)
            copies.append(
                pltpu.make_async_copy(array.at[snap], packs[j].at[:, cols], sems.at[i, j])
            )
    for copy in copies:
        copy.start()
    first = dom * nblk - 1
    acc[...] = jnp.zeros_like(acc)
    for b in range(nblk):
        rows = slice(b * bsize, (b + 1) * bsize)
        for k in range(width):
            used = (k < counts[b]).astype(F32)
            start = pl.multiple_of((sources[b, k] - first) * bsize, bsize)
            acc[rows, pl.ds(start, bsize)] += tiles[b, k].astype(F32) * used
    total = acc[...]
    dense = (total / jnp.sum(total, axis=1, keepdims=True)).astype(BF)
    for pack in packs:
        pack[:, :reach] = dense
    for copy in copies:
        copy.wait()


def pack_inputs(tiles, sources, counts, features, cotangent, doms):
    nblk, width, bsize, _ = tiles.shape
    _, span, feats = features.shape
    reach = (nblk + 2) * bsize
    chips = doms // 2
    smem = pl.BlockSpec(memory_space=pltpu.SMEM)
    anywhere = pl.BlockSpec(memory_space=pl.ANY)
    return pl.pallas_call(
        functools.partial(pack_kernel, doms),
        out_shape=[pltpu.VMEM((span, reach + 2 * feats), BF)] * chips,
        in_specs=[smem, smem, pl.BlockSpec(memory_space=pltpu.VMEM), anywhere, anywhere],
        out_specs=[pl.BlockSpec(memory_space=pltpu.VMEM)] * chips,
        scratch_shapes=[
            pltpu.VMEM((span, reach), F32),
            pltpu.SemaphoreType.DMA((2, chips)),
        ],
    )(
        sources,
        counts,
        tiles,
        pltpu.with_memory_space_constraint(features, pltpu.HBM),
        pltpu.with_memory_space_constraint(cotangent, pltpu.HBM),
    )


def step_kernel(doms, layers, count, bsize, *refs):
    packs = refs[:doms]
    pieces = refs[doms : doms + layers]
    (grads, adj, stage, weight, h_even, h_odd, nrm, slope, scale, dz, grad, sems) = refs[
        doms + layers :
    ]
    section, dom = lax.axis_index("section"), lax.axis_index("dom")
    span = adj.shape[1]
    reach = adj.shape[2]
    feats = h_even.shape[0]
    nodes = doms * span
    half = doms // 2
    late = (dom >= half).astype(jnp.int32)
    active = (lax.rem(dom, half) == 0) & (2 * section + late < count)

    @pl.when(jnp.logical_not(active))
    def _():
        grads[...] = jnp.zeros_like(grads)

    @pl.when(active)
    def _():
        f_copies, a_copies, c_copies, w_copies = [], [], [], []
        for j, pack in enumerate(packs):
            start = dom if j < half else lax.bitwise_xor(dom, 1)
            at = lax.rem(start + 2 * lax.rem(j, half), doms)
            rows = pl.ds(pl.multiple_of(at * span, span), span)
            feat = pack.at[:, pl.ds(reach, feats)]
            cot = pack.at[:, pl.ds(reach + feats, feats)]
            f_copies.append(pltpu.make_async_copy(feat, stage.at[0, rows], sems.at[0, j]))
            a_copies.append(
                pltpu.make_async_copy(pack.at[:, pl.ds(0, reach)], adj.at[at], sems.at[1, j])
            )
            c_copies.append(pltpu.make_async_copy(cot, stage.at[1, rows], sems.at[2, j]))
        for mask, piece in enumerate(pieces):
            slot = lax.bitwise_xor(section, mask)
            w_copies.append(
                pltpu.make_async_copy(piece.at[0], weight.at[slot], sems.at[3, mask])
            )
        for copy in f_copies + w_copies + a_copies + c_copies:
            copy.start()
        edge = jnp.zeros((feats, bsize), BF)
        for hidden in (h_even, h_odd):
            hidden[:, :bsize] = edge
            hidden[:, bsize + nodes :] = edge
        for copy in f_copies:
            copy.wait()
        h_even[:, bsize : bsize + nodes] = stage[0].T
        for copy in w_copies:
            copy.wait()
        for copy in a_copies:
            copy.wait()

        def forward_layers(base, size):
            steps = [(i, d) for i in range(size) for d in range(doms)]
            aggs, units, zvals, wts = {}, {}, {}, {}

            def bound(i):
                return (h_odd, h_even) if i % 2 else (h_even, h_odd)

            def gather(t):
                i, d = steps[t]
                src, _ = bound(i)
                aggs[t] = lax.dot_general(
                    src[:, d * span : d * span + reach], adj[d], NT, preferred_element_type=F32
                )

            def project(t):
                i, d = steps[t]
                cols = slice(d * span, (d + 1) * span)
                agg = aggs.pop(t)
                mean = jnp.sum(agg * agg, axis=0, keepdims=True) * (1.0 / feats)
                factor = lax.rsqrt(mean + epsilon)
                unit = (agg * factor).astype(BF)
                scale[base + i, :, cols] = factor
                nrm[base + i, :, cols] = unit
                if d == 0:
                    wts[i] = weight[base + i].T
                zvals[t] = jnp.dot(wts[i], unit, preferred_element_type=F32)

            def activate(t):
                i, d = steps[t]
                src, dst = bound(i)
                cols = slice(d * span, (d + 1) * span)
                own = slice(bsize + d * span, bsize + (d + 1) * span)
                z_val = zvals.pop(t)
                sig = 0.5 * jnp.tanh(0.5 * z_val) + 0.5
                act = z_val * sig
                slope[base + i, :, cols] = (sig + act * (1.0 - sig)).astype(BF)
                dst[:, own] = (src[:, own].astype(F32) + act).astype(BF)

            for t in range(len(steps) + 2):
                if 0 <= t - 2:
                    activate(t - 2)
                if t < len(steps):
                    gather(t)
                if 0 <= t - 1 < len(steps):
                    project(t - 1)

        def backward_layers(top, size, last):
            steps = [(i, d) for i in range(size) for d in range(doms)]
            dnrms, spreads = {}, {}

            def begin(t):
                i, d = steps[t]
                cols = slice(d * span, (d + 1) * span)
                value = (grad[:, cols] * slope[top - i, :, cols].astype(F32)).astype(BF)
                dz[i % 2, :, cols] = value
                if not (last and i == size - 1):
                    dnrms[t] = jnp.dot(weight[top - i], value, preferred_element_type=F32)

            def spread(t):
                i, d = steps[t]
                cols = slice(d * span, (d + 1) * span)
                dnrm = dnrms.pop(t)
                unit = nrm[top - i, :, cols].astype(F32)
                mean = jnp.sum(dnrm * unit, axis=0, keepdims=True) * (1.0 / feats)
                dagg = (scale[top - i, :, cols] * (dnrm - unit * mean)).astype(BF)
                spreads[t] = jnp.dot(dagg, adj[d], preferred_element_type=F32)

            def update(t):
                i, d = steps[t]
                mine = spreads[t]
                low = mine[:, bsize : 2 * bsize]
                high = mine[:, span : span + bsize]
                if d > 0:
                    low = low + spreads.pop(t - 1)[:, span + bsize :]
                if d < doms - 1:
                    high = high + spreads[t + 1][:, :bsize]
                at = d * span
                grad[:, at : at + bsize] += low
                if span > 2 * bsize:
                    grad[:, at + bsize : at + span - bsize] += mine[:, 2 * bsize : span]
                grad[:, at + span - bsize : at + span] += high

            def weigh(i):
                dweight = lax.dot_general(nrm[top - i], dz[i % 2], NT, preferred_element_type=F32)
                mask = lax.bitwise_xor(section, top - i)
                grads[lax.rem(mask, 2), lax.div(mask, 2)] = dweight.astype(BF)

            full = len(steps) - (doms if last else 0)
            for t in range(len(steps) + 2):
                if t and t % doms == 0 and t <= len(steps):
                    weigh(t // doms - 1)
                if t < len(steps):
                    begin(t)
                if 0 <= t - 1 < full:
                    spread(t - 1)
                if 0 <= t - 2 < full:
                    update(t - 2)

        small = layers * doms <= 32
        if small:
            forward_layers(0, layers)
        else:
            lax.fori_loop(0, layers // 2, lambda p, c: (forward_layers(2 * p, 2), c)[1], 0)
            if layers % 2:
                forward_layers(layers - 1, 1)

        for copy in c_copies:
            copy.wait()
        grad[...] = stage[1].astype(F32).T

        if small:
            backward_layers(layers - 1, layers, True)
        else:
            lax.fori_loop(
                0, layers - 1, lambda p, c: (backward_layers(layers - 1 - p, 1, False), c)[1], 0
            )
            backward_layers(0, 1, True)


def train_step(packs, pieces, count, bsize, feats):
    doms, layers = len(packs), len(pieces)
    span = packs[0].shape[0]
    reach = packs[0].shape[1] - 2 * feats
    nodes = doms * span
    padded = nodes + 2 * bsize
    anywhere = pl.BlockSpec(memory_space=pl.ANY)
    need = layers * feats * (4 * nodes + 32 * nodes // feats + 6 * feats) + 16 * 2**20
    need = min(need, 60 * 2**20)
    return pl.pallas_call(
        functools.partial(step_kernel, doms, layers, count, bsize),
        out_shape=jax.ShapeDtypeStruct((2, layers // 2, feats, feats), BF),
        in_specs=[anywhere] * (doms + layers),
        out_specs=pl.BlockSpec(memory_space=pltpu.VMEM),
        scratch_shapes=[
            pltpu.VMEM((doms, span, reach), BF),
            pltpu.VMEM((2, nodes, feats), BF),
            pltpu.VMEM((layers, feats, feats), BF),
            pltpu.VMEM((feats, padded), BF),
            pltpu.VMEM((feats, padded), BF),
            pltpu.VMEM((layers, feats, nodes), BF),
            pltpu.VMEM((layers, feats, nodes), BF),
            pltpu.VMEM((layers, 1, nodes), F32),
            pltpu.VMEM((2, feats, nodes), BF),
            pltpu.VMEM((feats, nodes), F32),
            pltpu.SemaphoreType.DMA((4, max(doms, layers))),
        ],
        compiler_params=pltpu.CompilerParams(vmem_limit_bytes=need),
    )(*packs, *pieces)


def local(features, cotangent, weights, tiles, sources, counts):
    count, span, feats = features.shape
    bsize = tiles.shape[-1]
    sections = lax.axis_size("section")
    doms = lax.axis_size("dom")
    section = lax.axis_index("section")
    dom = lax.axis_index("dom")
    core = lax.rem(dom, 2)
    chips = doms // 2
    wide = sections // 2

    def move(array, where):
        pairs = []
        for s in range(sections):
            for d in range(doms):
                to_s, to_d = where(s, d)
                pairs.append((s * doms + d, to_s * doms + to_d))
        return lax.ppermute(array, BOTH, pairs)

    def swap_core(array):
        return move(array, lambda s, d: (s, d ^ 1))

    def shift_chip(array, by):
        return move(array, lambda s, d: (s, (d - 2 * by) % doms))

    def even(r):
        return (2 * r + wide) % sections

    def odd(r):
        return 2 * r + 1

    def swap_round(array, r):
        def where(s, d):
            if d % 2:
                return s ^ odd(r), d
            return (s ^ even(r), d) if even(r) else (s, (d + 2) % doms)

        return move(array, where)

    arrived = [swap_round(weights, r) for r in range(wide)]
    packs = list(pack_inputs(tiles, sources, counts, features, cotangent, doms))
    packs = packs[:1] + [shift_chip(pack, j) for j, pack in enumerate(packs) if j]
    near = swap_core(packs[0])
    far, arrived = lax.optimization_barrier((packs[1:], arrived))
    packs = packs[:1] + far + [near] + [swap_core(pack) for pack in far]
    handed = [swap_core(piece) for piece in arrived]
    pieces = [weights] * sections
    for r in range(wide):
        if even(r):
            pieces[even(r)] = arrived[r]
        pieces[odd(r)] = handed[r]
    grads = train_step(packs, pieces, count, bsize, feats)

    held = grads[0] + swap_core(grads[1])
    total = jnp.where(core == 0, held[0].astype(F32), 0.0)
    for r in range(wide):
        slot = jnp.where(core == 0, even(r) // 2, odd(r) // 2)
        piece = lax.dynamic_index_in_dim(held, slot, 0, False)
        piece = swap_round(piece, r).astype(F32)
        total = total + (piece if even(r) else jnp.where(core == 0, 0.0, piece))
    gathered = lax.all_gather(total.astype(BF), "dom")
    result = jnp.sum(gathered.astype(F32), axis=0) * (1.0 / math.sqrt(count * span * doms))
    return result[None]


def solution(mesh):
    in_specs = (
        P(None, "dom", None),
        P(None, "dom", None),
        P("section", None, None),
        P("dom", None, None, None),
        P("dom", None),
        P("dom"),
    )
    out_specs = P("section", None, None)
    return jax.shard_map(local, mesh=mesh, in_specs=in_specs, out_specs=out_specs, check_vma=False)
```
